32 devices in a mesh: dp: 2 (over core), expert: 16 (over z, y, x).
Axes of the slice: x: 2, y: 2, z: 4, core: 2. Of those that a mesh axis runs over, the one named last changes fastest.
Arguments:
- tokens: bfloat16 [2048, 4096], P(('dp', 'expert')), may hold values from -6 to 6
- token_experts: int32 [2048, 8], P(('dp', 'expert')), may hold values from 0 to 15, all different within a row; in each aligned block of 64 rows (0 to 63, 64 to 127, ...) at most 48 rows name the same one
- hidden_grad: bfloat16 [2048, 8, 768], P(('dp', 'expert')), may hold values from -6 to 6
- held_expert: int32 [16], replicated, may hold values from 0 to 15, each once
- swap_mask: int32 [16], replicated, may hold values from 0 to 1, as said below
- weight: bfloat16 [16, 4096, 768], P('expert', 'dp'), may hold values from -0.09375 to 0.09375
- first_moment: float32 [16, 4096, 768], P('expert', 'dp'), may hold values from -57.6 to 57.6
- second_moment: float32 [16, 4096, 768], P('expert', 'dp'), may hold values from 10.24 to 102.4
Outputs:
- token_grad: bfloat16 [2048, 4096], P(('dp', 'expert'))
- adam_step: bfloat16 [16, 4096, 768], P('expert', 'dp')
The draws below stay inside these ranges and needn't reach their ends.
Inputs may be any that keep to these rules, and one draw needn't show every extreme that they name: `token_experts`: in each aligned block of 64 rows (the tokens of one device) no expert is named by more than 48 rows, and in some blocks one is named by exactly 48; the ids of a row differ. `held_expert`: a permutation of the expert ids. swap_mask[p] equals swap_mask[p + 8] for p below 8, and exactly 2 such pairs are 1.
All inputs are finite; a program needn't handle non-finite values.
Results may differ from the reference program's by a relative error of at most 0.008.
Values may be sent and summed in bfloat16 or wider, within the bound.
A program may use at most 128 MiB of HBM per device.

```python
import math
import jax
import jax.numpy as jnp
import numpy as np
from jax import lax

D = 4096
FF = 768
TOP = 8
TOK_DEV = 64
EXPERTS = 16
TOKENS = 2048
REPLICA_TOKENS = 1024
CAP = 48
SLOTS = 768
ROWS_EXPERT = 1024
SWAP_PAIRS = 2
N_DP = 2


def draw_swap_mask(key, part):
    half_count = EXPERTS // 2
    order = jax.random.permutation(key, half_count)
    lower = (order < SWAP_PAIRS).astype(jnp.int32)
    return jnp.concatenate([lower, lower])


def levels(key, dims, pieces, smallest, largest):
    def one(dim, shards_of):
        steps = jax.random.uniform(jax.random.fold_in(jax.random.fold_in(key, 6), dim), (shards_of,), jnp.float32, smallest / len(pieces), largest / len(pieces))
        return jnp.repeat(jnp.exp(steps), dims[dim] // shards_of).reshape((-1,) + (1,) * (len(dims) - dim - 1))

    gain = one(*pieces[0])
    for cut in pieces[1:]:
        gain = gain * one(*cut)
    return gain


def shared_out(own_key, own, number, rows, count, top, reach, slope):
    sequence = jax.random.permutation(own_key, count)
    crowded, common = shares(count, rows * top, reach, slope, True), shares(count, rows * top, reach, slope, False)
    places = jnp.arange(count)

    def named(tallies, rotation):
        used = int((tallies > 0).sum())
        fixed = max(1, used // 4)
        passed = fixed + (places - fixed + rotation * (used - fixed)) % max(1, count - fixed)
        return jnp.zeros((count,), jnp.int32).at[sequence[jnp.where(places < fixed, places, passed)]].set(jnp.asarray(tallies, jnp.int32))

    tallies = jnp.where(number % 4 == 0, named(crowded, number // 4), named(common, number - number // 4 - 1))
    mixed = jax.random.permutation(jax.random.fold_in(own, 3), count)
    donor, sink = mixed[0:count // 2 * 2:2], mixed[1:count // 2 * 2:2]
    margin = jnp.minimum(tallies[donor] - 1, reach - tallies[sink]) // 2
    margin = jnp.where((donor == sequence[0]) | (sink == sequence[0]) | (tallies[sink] == 0), 0, jnp.maximum(margin, 0))
    passed = jax.random.randint(jax.random.fold_in(own, 4), (count // 2,), 0, 1 << 20) % (margin + 1)
    tallies = tallies.at[donor].add(-passed).at[sink].add(passed)
    items = jnp.searchsorted(jnp.cumsum(tallies), jnp.arange(rows * top), side="right").astype(jnp.int32)
    table = items.reshape(top, rows).T
    table = table[jax.random.permutation(jax.random.fold_in(own, 1), rows)]
    rotation = jax.random.randint(jax.random.fold_in(own, 2), (rows, 1), 0, top)
    return jnp.take_along_axis(table, (jnp.arange(top)[None, :] + rotation) % top, axis=1)


def shares(count, total, limit, slope, full):
    portions = [(1 << 20) // math.isqrt(standing ** slope) + 1 for standing in range(1, count + 1)]
    largest = limit if full else min(limit, max(-(-total // count), total * portions[0] // sum(portions)))
    least = 1 if total - largest >= count - 1 else 0
    counts, rest = [largest] + [least] * (count - 1), total - largest - least * (count - 1)
    while rest > 0:
        movable = [i for i in range(1, count) if counts[i] < largest] or [i for i in range(1, count) if counts[i] < limit]
        whole, left = sum([portions[i] for i in movable]), rest
        for i in movable:
            addition = min(limit - counts[i], max(1, left * portions[i] // whole), rest)
            counts[i] = counts[i] + addition
            rest = rest - addition
    return np.array(counts)


def gaussian(rng, extent, spread, reach, split=(), kind=jnp.bfloat16):
    array = jax.random.normal(rng, extent, jnp.float32) * spread
    if len(split) > 0:
        array = levels(rng, extent, split, -0.22, 0.18) * array
    return jnp.clip(array, min=-reach, max=reach).astype(kind)


def setup_inputs(seed: int = 0) -> dict:
    seeds = jax.random.split(jax.random.key(seed), 9)
    tokens = gaussian(seeds[0], (TOKENS, D), 1.0, 6.0, ((0, 32),))
    token_experts_keys = jax.random.split(jax.random.fold_in(seeds[1], 1), TOKENS // TOK_DEV)
    token_experts_turns = jax.random.permutation(jax.random.fold_in(seeds[1], 3), TOKENS // TOK_DEV)
    token_experts = jax.vmap(lambda own, number: shared_out(jax.random.fold_in(seeds[1], 2), own, number, TOK_DEV, EXPERTS, TOP, CAP, 2))(token_experts_keys, token_experts_turns).reshape((TOKENS, TOP))
    hidden_grad = gaussian(seeds[2], (TOKENS, TOP, FF), 1.0, 6.0, ((0, 32),))
    held_expert = jax.random.permutation(seeds[3], EXPERTS).astype(jnp.int32)
    swap_mask = draw_swap_mask(jax.random.fold_in(seeds[8], 71), 0)
    weight = gaussian(seeds[5], (EXPERTS, D, FF), D ** -0.5, 0.09375, ((0, 16), (1, 2)))
    first_moment = gaussian(seeds[6], (EXPERTS, D, FF), (0.3 * ROWS_EXPERT ** 0.5), 57.6, ((0, 16), (1, 2)), jnp.float32)
    second_moment = jnp.clip(jnp.exp(math.log(102.4) - 2.3025851 * jax.random.uniform(seeds[7], (EXPERTS, D, FF), jnp.float32) ** levels(seeds[7], (EXPERTS, D, FF), ((0, 16), (1, 2)), -0.2, 0.2)), 10.24, 102.4)
    return {"tokens": tokens, "token_experts": token_experts, "hidden_grad": hidden_grad, "held_expert": held_expert, "swap_mask": swap_mask, "weight": weight, "first_moment": first_moment, "second_moment": second_moment}


def adam_direction(grad, first, second):
    first_new = 0.9 * first + 0.1 * grad
    second_new = 0.95 * second + 0.05 * grad * grad
    return (first_new / (jnp.sqrt(second_new) + 1e-08)).astype(jnp.bfloat16)

def reference(tokens, token_experts, hidden_grad, held_expert, swap_mask, weight, first_moment, second_moment):
    lanes = jnp.arange(EXPERTS, dtype=jnp.int32)
    partner = (lanes + EXPERTS // 2) % EXPERTS
    source_slot = jnp.where(swap_mask == 1, partner, lanes).astype(jnp.int32)
    new_held = held_expert[source_slot]
    slot_of = lax.optimization_barrier(jnp.sum(jnp.where(held_expert[None, :] == lanes[:, None], lanes[None, :], 0), axis=1)).astype(jnp.int32)
    width = tokens.shape[1]
    hidden = hidden_grad.shape[2]
    top = token_experts.shape[1]
    rep_tokens = tokens.reshape(N_DP, REPLICA_TOKENS, width)
    rep_ids = token_experts.reshape(N_DP, REPLICA_TOKENS, top)
    rep_grads = hidden_grad.reshape(N_DP, REPLICA_TOKENS, top, hidden)
    picks = jnp.arange(top, dtype=jnp.int32)
    slot_range = jnp.arange(SLOTS, dtype=jnp.int32)

    def step(carry, lane):
        expert_id = new_held[lane]
        full_w = weight[slot_of[expert_id]]
        total = jnp.zeros((width, hidden), jnp.float32)
        for rep in range(N_DP):
            hit_k = rep_ids[rep] == expert_id
            hit = jnp.any(hit_k, axis=1)
            kpos = lax.optimization_barrier(jnp.sum(jnp.where(hit_k, picks[None, :], 0), axis=1)).astype(jnp.int32)
            rows = jnp.nonzero(hit, size=SLOTS, fill_value=0)[0].astype(jnp.int32)
            count = jnp.sum(hit.astype(jnp.int32))
            valid = slot_range < count
            xs = rep_tokens[rep][rows]
            gs = rep_grads[rep][rows, kpos[rows]]
            gs = jnp.where(valid[:, None], gs, jnp.zeros_like(gs))
            pre = jnp.dot(xs, full_w, preferred_element_type=jnp.float32)
            sig = jax.nn.sigmoid(pre)
            grad_pre = (gs.astype(jnp.float32) * sig * (1.0 + pre * (1.0 - sig))).astype(jnp.bfloat16)
            row_grad = jnp.dot(grad_pre, full_w.T, preferred_element_type=jnp.float32).astype(jnp.bfloat16)
            carry = carry.at[rep, rows].add(row_grad.astype(jnp.float32))
            part = lax.dot_general(xs, grad_pre, (((0,), (0,)), ((), ())), preferred_element_type=jnp.float32)
            part = lax.optimization_barrier(part.astype(jnp.bfloat16))
            total = total + part.astype(jnp.float32)
        src = source_slot[lane]
        return (carry, adam_direction(total, first_moment[src], second_moment[src]))
    start = jnp.zeros((N_DP, REPLICA_TOKENS, width), jnp.float32)
    carry, adam_step = lax.scan(step, start, lanes)
    token_grad = carry.reshape(N_DP * REPLICA_TOKENS, width).astype(jnp.bfloat16)
    return (token_grad, adam_step)
```

```python
import itertools

import jax
import jax.numpy as jnp
from jax import lax
from jax.sharding import PartitionSpec as P


def adam_direction(grad, first, second):
    first_new = 0.9 * first + 0.1 * grad
    second_new = 0.95 * second + 0.05 * grad * grad
    return (first_new / (jnp.sqrt(second_new) + 1e-08)).astype(jnp.bfloat16)


def swap_slots(block, swap_mask, here):
    count = swap_mask.shape[0]
    half = count // 2
    pairs = max(1, count // 8)
    lower = swap_mask[:half]
    moving = jnp.sum(jnp.where(jnp.arange(count) == here, swap_mask, 0)) == 1
    choices = list(itertools.combinations(range(half), pairs)) if half <= 8 else None
    if choices is None:
        got = lax.ppermute(block, "expert", [(i, (i + half) % count) for i in range(count)])
        return jnp.where(moving, got, block)

    def branch(chosen):
        route = [(p, p + half) for p in chosen] + [(p + half, p) for p in chosen]

        def run(value):
            return jnp.where(moving, lax.ppermute(value, "expert", route), value)

        return run

    table = jnp.array([[int(p in c) for p in range(half)] for c in choices], jnp.int32)
    fits = jnp.all(table == lower[None, :], axis=1).astype(jnp.int32)
    number = jnp.sum(fits * jnp.arange(len(choices), dtype=jnp.int32))
    return lax.switch(number, [branch(c) for c in choices], block)


def body(
    tokens, token_experts, hidden_grad, held_expert, swap_mask, weight, first_moment, second_moment
):
    count_dev = lax.axis_size("expert")
    n_dp = lax.axis_size("dp")
    here = lax.axis_index("expert")
    row = lax.axis_index("dp")
    tok_dev, top = token_experts.shape
    hidden = hidden_grad.shape[2]
    rows_x = lax.all_gather(tokens, "expert", axis=0, tiled=True)
    full_w = lax.all_gather(weight[0], "dp", axis=0, tiled=True)
    named = token_experts[None, :, :] == held_expert[:, None, None]
    same = jnp.eye(tok_dev, dtype=jnp.bool_)
    place = (same[None, :, :, None] & named[:, None, :, :]).astype(jnp.bfloat16)
    send_g = jnp.dot(
        place.reshape(count_dev * tok_dev, tok_dev * top),
        hidden_grad.reshape(tok_dev * top, hidden),
        preferred_element_type=jnp.float32,
    ).astype(jnp.bfloat16)
    rows_g = lax.all_to_all(
        send_g.reshape(count_dev, tok_dev, hidden), "expert", split_axis=0, concat_axis=0, tiled=True
    ).reshape(count_dev * tok_dev, hidden)
    pre = jnp.dot(rows_x, full_w, preferred_element_type=jnp.float32)
    sig = jax.nn.sigmoid(pre)
    grad_pre = (rows_g.astype(jnp.float32) * sig * (1.0 + pre * (1.0 - sig))).astype(jnp.bfloat16)
    partial = lax.dot_general(
        rows_x, grad_pre, (((0,), (0,)), ((), ())), preferred_element_type=jnp.float32
    ).astype(jnp.bfloat16)
    if n_dp == 2:
        depth = partial.shape[0] // 2
        mine = lax.dynamic_slice_in_dim(partial, row * depth, depth, 0)
        other = lax.dynamic_slice_in_dim(partial, (1 - row) * depth, depth, 0)
        got = lax.ppermute(other, "dp", [(0, 1), (1, 0)])
        expert_grad = mine.astype(jnp.float32) + got.astype(jnp.float32)
    else:
        expert_grad = lax.psum_scatter(
            partial, "dp", scatter_dimension=0, tiled=True
        ).astype(jnp.float32)
    back_rows = lax.dot_general(
        grad_pre, full_w, (((1,), (1,)), ((), ())), preferred_element_type=jnp.float32
    ).astype(jnp.bfloat16)
    token_grad = lax.psum_scatter(back_rows, "expert", scatter_dimension=0, tiled=True)
    adam_step = adam_direction(expert_grad, first_moment[0], second_moment[0])
    adam_step = swap_slots(adam_step, swap_mask, here)[None]
    return (token_grad, adam_step)


def solution(mesh):
    in_specs = (
        P(("dp", "expert"), None),
        P(("dp", "expert"), None),
        P(("dp", "expert"), None, None),
        P(),
        P(),
        P("expert", "dp", None),
        P("expert", "dp", None),
        P("expert", "dp", None),
    )
    out_specs = (P(("dp", "expert"), None), P("expert", "dp", None))
    return jax.shard_map(body, mesh=mesh, in_specs=in_specs, out_specs=out_specs, check_vma=False)
```

```python
import itertools

import jax
import jax.numpy as jnp
from jax import lax
from jax.sharding import PartitionSpec as P


def adam_direction(grad, first, second):
    first_new = 0.9 * first + 0.1 * grad
    second_new = 0.95 * second + 0.05 * grad * grad
    return (first_new / (jnp.sqrt(second_new) + 1e-08)).astype(jnp.bfloat16)


def swap_slots(block, swap_mask, here):
    count = swap_mask.shape[0]
    half = count // 2
    pairs = max(1, count // 8)
    lower = swap_mask[:half]
    moving = jnp.sum(jnp.where(jnp.arange(count) == here, swap_mask, 0)) == 1
    choices = list(itertools.combinations(range(half), pairs)) if half <= 8 else None
    if choices is None:
        got = lax.ppermute(block, "expert", [(i, (i + half) % count) for i in range(count)])
        return jnp.where(moving, got, block)

    def branch(chosen):
        route = [(p, p + half) for p in chosen] + [(p + half, p) for p in chosen]

        def run(value):
            return jnp.where(moving, lax.ppermute(value, "expert", route), value)

        return run

    table = jnp.array([[int(p in c) for p in range(half)] for c in choices], jnp.int32)
    fits = jnp.all(table == lower[None, :], axis=1).astype(jnp.int32)
    number = jnp.sum(fits * jnp.arange(len(choices), dtype=jnp.int32))
    return lax.switch(number, [branch(c) for c in choices], block)


def exchange(block, bit, count):
    return lax.ppermute(block, "expert", [(i, i ^ bit) for i in range(count)])


CHUNKS = ((13, (8, 4, 1, 2)), (13, (8, 4, 2, 1)), (6, (1, 2, 8, 4)))


def column_chunks(width):
    unit, start = width // sum(size for size, _ in CHUNKS), 0
    for size, order in CHUNKS:
        yield start, start + size * unit, order
        start += size * unit


def axes_by_bit(order):
    crossed = order[::-1]
    return tuple(crossed.index(bit) for bit in (8, 4, 2, 1))


def gather_rows(tokens, count):
    rows, width = tokens.shape
    parts = []
    for start, stop, order in column_chunks(width):
        held = tokens[:, start:stop]
        for bit in order:
            held = jnp.concatenate([held, exchange(held, bit, count)], axis=0)
        held = held.reshape(2, 2, 2, 2, rows, stop - start)
        held = held.transpose(*axes_by_bit(order), 4, 5)
        parts.append(held.reshape(count * rows, stop - start))
    return jnp.concatenate(parts, axis=1)


def scatter_sums(grad_pre, full_w, count):
    rows = grad_pre.shape[0] // count
    parts = []
    for start, stop, order in column_chunks(full_w.shape[0]):
        product = lax.dot_general(
            grad_pre,
            full_w[start:stop],
            (((1,), (1,)), ((), ())),
            preferred_element_type=jnp.float32,
        ).astype(jnp.bfloat16)
        held = product.reshape(2, 2, 2, 2, rows, stop - start)
        left = [8, 4, 2, 1]
        for bit in order[::-1]:
            axis = left.index(bit)
            left.remove(bit)
            keep = lax.index_in_dim(held, 0, axis, keepdims=False)
            away = lax.index_in_dim(held, 1, axis, keepdims=False)
            shape = away.shape
            got = exchange(away.reshape(-1, stop - start), bit, count).reshape(shape)
            held = (keep.astype(jnp.float32) + got.astype(jnp.float32)).astype(jnp.bfloat16)
        parts.append(held)
    return jnp.concatenate(parts, axis=1)


def body(
    tokens, token_experts, hidden_grad, held_expert, swap_mask, weight, first_moment, second_moment
):
    count_dev = lax.axis_size("expert")
    n_dp = lax.axis_size("dp")
    here = lax.axis_index("expert")
    row = lax.axis_index("dp")
    tok_dev, top = token_experts.shape
    hidden = hidden_grad.shape[2]
    by_bits = count_dev == 16
    if by_bits:
        rows_x = gather_rows(tokens, count_dev)
    else:
        rows_x = lax.all_gather(tokens, "expert", axis=0, tiled=True)
    full_w = lax.all_gather(weight[0], "dp", axis=0, tiled=True)
    named = token_experts[None, :, :] == held_expert[:, None, None]
    same = jnp.eye(tok_dev, dtype=jnp.bool_)
    place = (same[None, :, :, None] & named[:, None, :, :]).astype(jnp.bfloat16)
    send_g = jnp.dot(
        place.reshape(count_dev * tok_dev, tok_dev * top),
        hidden_grad.reshape(tok_dev * top, hidden),
        preferred_element_type=jnp.float32,
    ).astype(jnp.bfloat16)
    rows_g = lax.all_to_all(
        send_g.reshape(count_dev, tok_dev, hidden), "expert", split_axis=0, concat_axis=0, tiled=True
    )
    if by_bits:
        rows_g = jnp.concatenate(
            [lax.dynamic_slice_in_dim(rows_g, here ^ r, 1, axis=0) for r in range(count_dev)], axis=0
        )
    rows_g = rows_g.reshape(count_dev * tok_dev, hidden)
    pre = jnp.dot(rows_x, full_w, preferred_element_type=jnp.float32)
    sig = jax.nn.sigmoid(pre)
    grad_pre = (rows_g.astype(jnp.float32) * sig * (1.0 + pre * (1.0 - sig))).astype(jnp.bfloat16)
    partial = lax.dot_general(
        rows_x, grad_pre, (((0,), (0,)), ((), ())), preferred_element_type=jnp.float32
    ).astype(jnp.bfloat16)
    if n_dp == 2:
        depth = partial.shape[0] // 2
        mine = lax.dynamic_slice_in_dim(partial, row * depth, depth, 0)
        other = lax.dynamic_slice_in_dim(partial, (1 - row) * depth, depth, 0)
        got = lax.ppermute(other, "dp", [(0, 1), (1, 0)])
        expert_grad = mine.astype(jnp.float32) + got.astype(jnp.float32)
    else:
        expert_grad = lax.psum_scatter(
            partial, "dp", scatter_dimension=0, tiled=True
        ).astype(jnp.float32)
    if by_bits:
        token_grad = scatter_sums(grad_pre, full_w, count_dev)
    else:
        back_rows = lax.dot_general(
            grad_pre, full_w, (((1,), (1,)), ((), ())), preferred_element_type=jnp.float32
        ).astype(jnp.bfloat16)
        token_grad = lax.psum_scatter(back_rows, "expert", scatter_dimension=0, tiled=True)
    adam_step = adam_direction(expert_grad, first_moment[0], second_moment[0])
    adam_step = swap_slots(adam_step, swap_mask, here)[None]
    return (token_grad, adam_step)


def solution(mesh):
    in_specs = (
        P(("dp", "expert"), None),
        P(("dp", "expert"), None),
        P(("dp", "expert"), None, None),
        P(),
        P(),
        P("expert", "dp", None),
        P("expert", "dp", None),
        P("expert", "dp", None),
    )
    out_specs = (P(("dp", "expert"), None), P("expert", "dp", None))
    return jax.shard_map(body, mesh=mesh, in_specs=in_specs, out_specs=out_specs, check_vma=False)
```

```python
import itertools

import jax
import jax.numpy as jnp
from jax import lax
from jax.sharding import PartitionSpec as P


def adam_direction(grad, first, second):
    first_new = 0.9 * first + 0.1 * grad
    second_new = 0.95 * second + 0.05 * grad * grad
    return (first_new / (jnp.sqrt(second_new) + 1e-08)).astype(jnp.bfloat16)


def swap_slots(block, swap_mask, here, sums, finish):
    count = swap_mask.shape[0]
    half = count // 2
    pairs = max(1, count // 8)
    lower = swap_mask[:half]
    moving = jnp.sum(jnp.where(jnp.arange(count) == here, swap_mask, 0)) == 1
    choices = list(itertools.combinations(range(half), pairs)) if half <= 8 else None
    if choices is None:
        got = lax.ppermute(block, "expert", [(i, (i + half) % count) for i in range(count)])
        return jnp.where(moving, got, block), finish(sums)

    def branch(chosen):
        route = [(p, p + half) for p in chosen] + [(p + half, p) for p in chosen]

        def run(value, sums):
            got = lax.ppermute(value, "expert", route)
            return jnp.where(moving, got, value), finish(sums)

        return run

    table = jnp.array([[int(p in c) for p in range(half)] for c in choices], jnp.int32)
    fits = jnp.all(table == lower[None, :], axis=1).astype(jnp.int32)
    number = jnp.sum(fits * jnp.arange(len(choices), dtype=jnp.int32))
    return lax.switch(number, [branch(c) for c in choices], block, sums)


CHUNKS = ((13, (2, 1, 4, 8)), (13, (1, 2, 4, 8)), (6, (8, 4, 2, 1)))


def cross(held, left, bit, here, count):
    axis = left.index(bit)
    side = (here // bit) % 2
    keep = lax.dynamic_index_in_dim(held, side, axis, keepdims=False)
    away = lax.dynamic_index_in_dim(held, 1 - side, axis, keepdims=False)
    route = [(i, i ^ bit) for i in range(count)]
    got = lax.ppermute(away.reshape(-1, away.shape[-1]), "expert", route).reshape(away.shape)
    total = (keep.astype(jnp.float32) + got.astype(jnp.float32)).astype(jnp.bfloat16)
    return total, [b for b in left if b != bit]


def first_sums(grad_pre, full_w, here, count):
    width = full_w.shape[0]
    unit, start = width // sum(size for size, _ in CHUNKS), 0
    rows = grad_pre.shape[0] // count
    sums = []
    for size, order in CHUNKS:
        stop = start + size * unit
        product = lax.dot_general(
            grad_pre,
            full_w[start:stop],
            (((1,), (1,)), ((), ())),
            preferred_element_type=jnp.float32,
        ).astype(jnp.bfloat16)
        held = product.reshape(2, 2, 2, 2, rows, stop - start)
        sums.append(cross(held, [8, 4, 2, 1], order[0], here, count)[0])
        start = stop
    return tuple(sums)


def later_sums(sums, here, count):
    parts = []
    for held, (_, order) in zip(sums, CHUNKS):
        left = [b for b in (8, 4, 2, 1) if b != order[0]]
        for bit in order[1:]:
            held, left = cross(held, left, bit, here, count)
        parts.append(held)
    return jnp.concatenate(parts, axis=1)


def body(
    tokens, token_experts, hidden_grad, held_expert, swap_mask, weight, first_moment, second_moment
):
    count_dev = lax.axis_size("expert")
    n_dp = lax.axis_size("dp")
    here = lax.axis_index("expert")
    row = lax.axis_index("dp")
    tok_dev, top = token_experts.shape
    hidden = hidden_grad.shape[2]
    rows_x = lax.all_gather(tokens, "expert", axis=0, tiled=True)
    full_w = lax.all_gather(weight[0], "dp", axis=0, tiled=True)
    named = token_experts[None, :, :] == held_expert[:, None, None]
    same = jnp.eye(tok_dev, dtype=jnp.bool_)
    place = (same[None, :, :, None] & named[:, None, :, :]).astype(jnp.bfloat16)
    send_g = jnp.dot(
        place.reshape(count_dev * tok_dev, tok_dev * top),
        hidden_grad.reshape(tok_dev * top, hidden),
        preferred_element_type=jnp.float32,
    ).astype(jnp.bfloat16)
    rows_g = lax.all_to_all(
        send_g.reshape(count_dev, tok_dev, hidden), "expert", split_axis=0, concat_axis=0, tiled=True
    ).reshape(count_dev * tok_dev, hidden)
    pre = jnp.dot(rows_x, full_w, preferred_element_type=jnp.float32)
    sig = jax.nn.sigmoid(pre)
    grad_pre = (rows_g.astype(jnp.float32) * sig * (1.0 + pre * (1.0 - sig))).astype(jnp.bfloat16)
    partial = lax.dot_general(
        rows_x, grad_pre, (((0,), (0,)), ((), ())), preferred_element_type=jnp.float32
    ).astype(jnp.bfloat16)
    if n_dp == 2:
        depth = partial.shape[0] // 2
        mine = lax.dynamic_slice_in_dim(partial, row * depth, depth, 0)
        other = lax.dynamic_slice_in_dim(partial, (1 - row) * depth, depth, 0)
        got = lax.ppermute(other, "dp", [(0, 1), (1, 0)])
        expert_grad = mine.astype(jnp.float32) + got.astype(jnp.float32)
    else:
        expert_grad = lax.psum_scatter(
            partial, "dp", scatter_dimension=0, tiled=True
        ).astype(jnp.float32)
    adam_step = adam_direction(expert_grad, first_moment[0], second_moment[0])
    if count_dev == 16:
        sums = first_sums(grad_pre, full_w, here, count_dev)

        def finish(values):
            return later_sums(values, here, count_dev)

    else:
        sums = lax.dot_general(
            grad_pre, full_w, (((1,), (1,)), ((), ())), preferred_element_type=jnp.float32
        ).astype(jnp.bfloat16)

        def finish(values):
            return lax.psum_scatter(values, "expert", scatter_dimension=0, tiled=True)

    adam_step, token_grad = swap_slots(adam_step, swap_mask, here, sums, finish)
    adam_step = adam_step[None]
    return (token_grad, adam_step)


def solution(mesh):
    in_specs = (
        P(("dp", "expert"), None),
        P(("dp", "expert"), None),
        P(("dp", "expert"), None, None),
        P(),
        P(),
        P("expert", "dp", None),
        P("expert", "dp", None),
        P("expert", "dp", None),
    )
    out_specs = (P(("dp", "expert"), None), P("expert", "dp", None))
    return jax.shard_map(body, mesh=mesh, in_specs=in_specs, out_specs=out_specs, check_vma=False)
```
